32 devices in a mesh: groups: 2 (over y), expert: 2 (over core), tensor: 8 (over z, x).
Axes of the slice: x: 2, y: 2, z: 4, core: 2. Of those that a mesh axis runs over, the one named last changes fastest.
Arguments:
- tokens: bfloat16 [384, 5120], P(('groups', 'expert')), parts along dimension 0, may hold values from -6 to 6
- router_score: bfloat16 [384], P(('groups', 'expert')), parts along dimension 0, may hold values from -6 to 6
- expert_ids: int32 [384, 1], P(('groups', 'expert')), parts along dimension 0, may hold values from 0 to 1; in each aligned block of 96 rows (0 to 95, 96 to 191, ...) at most 64 rows name the same one
- gate_up: bfloat16 [2, 5120, 16384], P('expert', None, 'tensor'), may hold values from -0.078125 to 0.078125
- down: bfloat16 [2, 8192, 5120], P('expert', 'tensor'), may hold values from -0.0625 to 0.0625
- shared_gate_up: bfloat16 [5120, 8192], P(None, 'tensor'), may hold values from -0.078125 to 0.078125
- shared_down: bfloat16 [4096, 5120], P('tensor'), may hold values from -0.09375 to 0.09375
Outputs:
- mixed: bfloat16 [384, 5120], P(('groups', 'expert')), parts along dimension 0
The draws below stay inside these ranges and needn't reach their ends.
There are 2 independent parts, one for each index of `groups`. The reference program is written for one: setup_inputs(seed, part) draws one part's arguments, and reference() takes and returns one part's arrays. A program takes and returns all parts, laid end to end along the dimension named above; an argument that names none is the same for every part. Nothing has to cross between parts.
Inputs may be any that keep to these rules, and one draw needn't show every extreme that they name: `expert_ids`: within the 96 rows of one index of expert no expert is chosen by more than 64 rows, a bound that some block reaches.
All inputs are finite; a program needn't handle non-finite values.
Results may differ from the reference program's by a relative error of at most 0.0052.
Values may be sent and summed in bfloat16 or wider, within the bound.
A program may use at most 128 MiB of HBM per device.

```python
import math
import jax
import jax.numpy as jnp
import numpy as np

D = 5120
FF = 8192
SF = 4096
CAP = 64
TOK_DEV = 96
TOKENS = 192
EXPERTS = 2
N_TENSOR = 8


def steps_of(own_key, shape, split, least, largest):
    gain = 1.0
    for position, parts in split:
        draws = jax.random.uniform(jax.random.fold_in(jax.random.fold_in(own_key, 6), position), (parts,), jnp.float32, least / len(split), largest / len(split))
        gain = gain * jnp.repeat(jnp.exp(draws), shape[position] // parts).reshape((-1,) + (1,) * (len(shape) - 1 - position))
    return gain


def routed_block(rng, own, number, rows, number_of, top, bound, slope):
    order = jax.random.permutation(rng, number_of)
    crowded, ordinary = load_shares(number_of, rows * top, bound, slope, True), load_shares(number_of, rows * top, bound, slope, False)
    places = jnp.arange(number_of)

    def named(sizes, rotation):
        used = int((sizes > 0).sum())
        fixed = max(1, used // 4)
        moved = fixed + (places - fixed + rotation * (used - fixed)) % max(1, number_of - fixed)
        return jnp.zeros((number_of,), jnp.int32).at[order[jnp.where(places < fixed, places, moved)]].set(jnp.asarray(sizes, jnp.int32))

    sizes = jnp.where(number % 4 == 0, named(crowded, number // 4), named(ordinary, number - number // 4 - 1))
    mixed = jax.random.permutation(jax.random.fold_in(own, 3), number_of)
    giver, sink = mixed[0:number_of // 2 * 2:2], mixed[1:number_of // 2 * 2:2]
    slack = jnp.minimum(sizes[giver] - 1, bound - sizes[sink]) // 2
    slack = jnp.where((giver == order[0]) | (sink == order[0]) | (sizes[sink] == 0), 0, jnp.maximum(slack, 0))
    moved = jax.random.randint(jax.random.fold_in(own, 4), (number_of // 2,), 0, 1 << 20) % (slack + 1)
    sizes = sizes.at[giver].add(-moved).at[sink].add(moved)
    labels = jnp.searchsorted(jnp.cumsum(sizes), jnp.arange(rows * top), side="right").astype(jnp.int32)
    table = labels.reshape(top, rows).T
    table = table[jax.random.permutation(jax.random.fold_in(own, 1), rows)]
    rotation = jax.random.randint(jax.random.fold_in(own, 2), (rows, 1), 0, top)
    return jnp.take_along_axis(table, (jnp.arange(top)[None, :] + rotation) % top, axis=1)


def load_shares(number_of, total, reach, slope, full):
    loads = [(1 << 20) // math.isqrt(rank ** slope) + 1 for rank in range(1, number_of + 1)]
    largest = reach if full else min(reach, max(-(-total // number_of), total * loads[0] // sum(loads)))
    least = 1 if total - largest >= number_of - 1 else 0
    holding, surplus = [largest] + [least] * (number_of - 1), total - largest - least * (number_of - 1)
    while surplus > 0:
        movable = [i for i in range(1, number_of) if holding[i] < largest] or [i for i in range(1, number_of) if holding[i] < reach]
        mass, budget = sum([loads[i] for i in movable]), surplus
        for i in movable:
            more = min(reach - holding[i], max(1, budget * loads[i] // mass), surplus)
            holding[i] = holding[i] + more
            surplus = surplus - more
    return np.array(holding)


def bell_draw(rng, shape, scale, bound, split=(), held_as=jnp.bfloat16):
    array = scale * jax.random.normal(rng, shape, jnp.float32)
    if split:
        array = array * steps_of(rng, shape, split, -0.22, 0.18)
    return jnp.clip(array, -bound, bound).astype(held_as)


def setup_inputs(seed: int = 0, part: int = 0) -> dict:
    key_of = jax.random.split(jax.random.key(seed), 8)
    own_keys = jax.random.split(jax.random.fold_in(key_of[7], part), 8)
    tokens = bell_draw(own_keys[0], (TOKENS, D), 1.0, 6.0, ((0, 2),))
    router_score = bell_draw(own_keys[1], (TOKENS,), 2.0, 6.0, ((0, 2),))
    expert_ids_keys = jax.random.split(jax.random.fold_in(own_keys[2], 1), TOKENS // TOK_DEV)
    expert_ids_turns = jax.random.permutation(jax.random.fold_in(own_keys[2], 3), TOKENS // TOK_DEV)
    expert_ids = jax.vmap(lambda own, number: routed_block(jax.random.fold_in(own_keys[2], 2), own, number, TOK_DEV, EXPERTS, 1, CAP, 2))(expert_ids_keys, expert_ids_turns).reshape((TOKENS, 1))
    gate_up = bell_draw(key_of[3], (EXPERTS, D, 2 * FF), D ** -0.5, 0.078125, ((0, 2), (2, 8)))
    down = bell_draw(key_of[4], (EXPERTS, FF, D), FF ** -0.5, 0.0625, ((0, 2), (1, 8)))
    shared_gate_up = bell_draw(key_of[5], (D, 2 * SF), D ** -0.5, 0.078125, ((1, 8),))
    shared_down = bell_draw(key_of[6], (SF, D), SF ** -0.5, 0.09375, ((0, 8),))
    return {"tokens": tokens, "router_score": router_score, "expert_ids": expert_ids, "gate_up": gate_up, "down": down, "shared_gate_up": shared_gate_up, "shared_down": shared_down}


def unpack_layout(weights, hidden):
    blocks = weights.reshape(weights.shape[0], N_TENSOR, 2, hidden // N_TENSOR)
    gate_part = blocks[:, :, 0, :].reshape(weights.shape[0], hidden)
    up_part = blocks[:, :, 1, :].reshape(weights.shape[0], hidden)
    return gate_part, up_part


def hidden_units(inputs, weights, hidden):
    gate_part, up_part = unpack_layout(weights, hidden)
    gate_val = jnp.dot(inputs, gate_part, preferred_element_type=jnp.float32)
    up_val = jnp.dot(inputs, up_part, preferred_element_type=jnp.float32)
    return (jax.nn.silu(gate_val) * up_val).astype(jnp.bfloat16)


def reference(tokens, router_score, expert_ids, gate_up, down, shared_gate_up, shared_down):
    factor = jax.nn.sigmoid(router_score.astype(jnp.float32))[:, None]
    scaled = (tokens.astype(jnp.float32) * factor).astype(jnp.bfloat16)
    shared_hidden = hidden_units(tokens, shared_gate_up, SF)
    total = jnp.dot(shared_hidden, shared_down, preferred_element_type=jnp.float32)
    for expert in range(EXPERTS):
        routed_hidden = hidden_units(scaled, gate_up[expert], FF)
        term = jnp.dot(routed_hidden, down[expert], preferred_element_type=jnp.float32)
        total = total + jnp.where(expert_ids[:, 0:1] == expert, term, jnp.float32(0.0))
    return total.astype(jnp.bfloat16)
```

```python
import jax
import jax.numpy as jnp
from jax import lax
from jax.experimental import pallas as pl
from jax.experimental.pallas import tpu as pltpu
from jax.sharding import PartitionSpec as P

CAP = 64
MESH = pl.DeviceIdType.MESH
UNITS = 256
WIDE = 1024
NZ, NX = 4, 2


def fused_kernel(
    tok_ref, score_ref, ids_ref, gu_ref, down_ref, sgu_ref, sdown_ref, out_ref,
    w1, w2, lhs, aux, hidden, part, core_out, core_in, xsum, x_out, x_in, zsum, z_out, z_in,
    w1_sem, w2_sem, tok_sem, tok_send, tok_recv,
    core_send, core_recv, x_send, x_recv, z_send, z_recv, gz_send, gz_recv, gx_send, gx_recv,
):
    rows, width = tok_ref.shape
    half = rows // NX
    routed = gu_ref.shape[1] // 2
    shared = sgu_ref.shape[1] // 2
    own_shared = shared // 2
    first_steps = w1.shape[0]
    chunks = w2.shape[0]
    piece = WIDE // NZ
    me = lax.axis_index("expert")
    tensor = lax.axis_index("tensor")
    z, x = tensor // NX, lax.rem(tensor, NX)
    core = {"expert": 1 - me}
    xpeer = {"tensor": z * NX + 1 - x}
    zpeer = [{"tensor": lax.rem(z + d, NZ) * NX + x} for d in range(1, NZ)]

    def w1_copies(j):
        if j == 0:
            at = pl.multiple_of(me * own_shared, own_shared)
            pair = (sgu_ref.at[:, pl.ds(at, UNITS)], sgu_ref.at[:, pl.ds(shared + at, UNITS)])
        else:
            at = (j - 1) * UNITS
            pair = (gu_ref.at[:, pl.ds(at, UNITS)], gu_ref.at[:, pl.ds(routed + at, UNITS)])
        return [
            pltpu.make_async_copy(src, w1.at[j, :, pl.ds(i * UNITS, UNITS)], w1_sem.at[j, i])
            for i, src in enumerate(pair)
        ]

    def w2_copies(c):
        cols = pl.ds(c * WIDE, WIDE)
        at = pl.multiple_of(me * own_shared, own_shared)
        return [
            pltpu.make_async_copy(down_ref.at[:, cols], w2.at[c, pl.ds(0, routed)], w2_sem.at[c, 0]),
            pltpu.make_async_copy(
                sdown_ref.at[pl.ds(at, own_shared), cols],
                w2.at[c, pl.ds(routed, own_shared)],
                w2_sem.at[c, 1],
            ),
        ]

    own_tok = pltpu.make_async_copy(tok_ref, lhs.at[0, pl.ds(0, rows)], tok_sem.at[0])
    own_tok.start()
    for j in range(first_steps):
        for copy in w1_copies(j):
            copy.start()
    for c in range(chunks):
        for copy in w2_copies(c):
            copy.start()

    score = score_ref[...].astype(jnp.float32)
    diagonal = lax.broadcasted_iota(jnp.int32, (rows, rows), 0) == lax.broadcasted_iota(
        jnp.int32, (rows, rows), 1
    )
    score = jnp.sum(jnp.where(diagonal, score, 0.0), axis=1, keepdims=True)
    factor = 1.0 / (1.0 + jnp.exp(-score))
    lane = lax.broadcasted_iota(jnp.int32, (rows, 128), 1)
    aux[0] = jnp.where(lane == 0, factor, ids_ref[...].astype(jnp.float32))

    barrier = pltpu.get_barrier_semaphore()
    for peer in [core, xpeer] + zpeer:
        pl.semaphore_signal(barrier, inc=1, device_id=peer, device_id_type=MESH)
    pl.semaphore_wait(barrier, 1 + 1 + NZ - 1)

    def remote(src, dst, send, recv, peer):
        return pltpu.make_async_remote_copy(
            src_ref=src, dst_ref=dst, send_sem=send, recv_sem=recv, device_id=peer,
            device_id_type=MESH,
        )

    tok_copy = remote(tok_ref, lhs.at[0, pl.ds(rows, rows)], tok_send.at[0], tok_recv.at[0], core)
    aux_copy = remote(aux.at[0], aux.at[1], tok_send.at[1], tok_recv.at[1], core)
    aux_copy.start()
    tok_copy.start()

    def scale(which):
        col = aux[which, :, 0:1]

        def body(i, carry):
            cols = pl.ds(pl.multiple_of(i * 512, 512), 512)
            at = pl.ds(which * rows, rows)
            lhs[1, at, cols] = (lhs[0, at, cols].astype(jnp.float32) * col).astype(jnp.bfloat16)
            return carry

        lax.fori_loop(0, width // 512, body, 0)

    own_tok.wait()
    scale(0)
    aux_copy.wait()
    tok_copy.wait()
    scale(1)

    mine = jnp.concatenate([aux[0, :, 1:2], aux[1, :, 1:2]], axis=0) == me.astype(jnp.float32)

    def first(j, carry):
        for i in range(2):
            block = w1.at[j, :, pl.ds(i * UNITS, UNITS)]
            pltpu.make_async_copy(block, block, w1_sem.at[j, i]).wait()
        both = jnp.dot(lhs[jnp.minimum(j, 1)], w1[j], preferred_element_type=jnp.float32)
        gate, up = both[:, :UNITS], both[:, UNITS:]
        unit = gate / (1.0 + jnp.exp(-gate)) * up
        unit = jnp.where(jnp.logical_or(mine, j == 0), unit, 0.0)
        hidden[j] = unit.astype(jnp.bfloat16)
        return carry

    lax.fori_loop(0, first_steps, first, 0)

    def core_copy(c):
        return remote(core_out.at[c], core_in.at[c], core_send.at[c], core_recv.at[c], core)

    def x_copy(c):
        return remote(x_out.at[c], x_in.at[c], x_send.at[c], x_recv.at[c], xpeer)

    def z_copy(c, d):
        there = lax.rem(z + d, NZ)
        return remote(
            z_out.at[c, there], z_in.at[c, d - 1], z_send.at[c, d - 1], z_recv.at[c, d - 1],
            zpeer[d - 1],
        )

    def columns(c, source):
        return pl.ds(pl.multiple_of(c * WIDE + source * piece, piece), piece)

    def gz_copy(c, d, source):
        block = out_ref.at[x, :, columns(c, source)]
        return remote(block, block, gz_send.at[c, d - 1], gz_recv.at[c, d - 1], zpeer[d - 1])

    def gx_copy(c, side):
        block = out_ref.at[side, :, pl.ds(pl.multiple_of(c * WIDE, WIDE), WIDE)]
        return remote(block, block, gx_send.at[c], gx_recv.at[c], xpeer)

    def second(c):
        for i, (at, size) in enumerate(((0, routed), (routed, own_shared))):
            block = w2.at[c, pl.ds(at, size)]
            pltpu.make_async_copy(block, block, w2_sem.at[c, i]).wait()
        for n in range(WIDE // 512):
            cols = pl.ds(n * 512, 512)
            total = None
            for j in range(first_steps):
                at = routed if j == 0 else (j - 1) * UNITS
                term = jnp.dot(
                    hidden[j], w2[c, pl.ds(at, UNITS), cols], preferred_element_type=jnp.float32
                )
                total = term if total is None else total + term
            part[c, :, cols] = total[:rows]
            core_out[c, :, cols] = total[rows:].astype(jnp.bfloat16)
        core_copy(c).start()

    def join_cores(c):
        core_copy(c).wait_recv()
        total = part[c] + core_in[c].astype(jnp.float32)
        xsum[0] = total[:half]
        xsum[1] = total[half:]
        zsum[c] = xsum[x]
        x_out[c] = xsum[1 - x].astype(jnp.bfloat16)
        x_copy(c).start()

    def join_x(c):
        x_copy(c).wait_recv()
        total = zsum[c] + x_in[c].astype(jnp.float32)
        zsum[c] = total
        for k in range(NZ):
            z_out[c, k] = total[:, k * piece:(k + 1) * piece].astype(jnp.bfloat16)
        for d in (2, 1, 3):
            z_copy(c, d).start()

    def join_z(c):
        total = zsum[c, :, pl.ds(pl.multiple_of(z * piece, piece), piece)]
        for d in range(1, NZ):
            z_copy(c, d).wait_recv()
            total = total + z_in[c, d - 1].astype(jnp.float32)
        out_ref[x, :, columns(c, z)] = total.astype(jnp.bfloat16)
        for d in (2, 1, 3):
            gz_copy(c, d, z).start()

    def pass_x(c):
        for d in range(1, NZ):
            gz_copy(c, d, lax.rem(z + NZ - d, NZ)).wait_recv()
        gx_copy(c, x).start()

    stages = ((0, second), (1, join_cores), (3, join_x), (4, join_z), (5, pass_x))

    def step(s, carry):
        for lag, stage in stages:
            c = s - lag

            @pl.when(jnp.logical_and(c >= 0, c < chunks))
            def _(stage=stage, c=c):
                stage(c)

        return carry

    lax.fori_loop(0, chunks + stages[-1][0], step, 0)

    def finish(c, carry):
        gx_copy(c, 1 - x).wait_recv()
        gx_copy(c, x).wait_send()
        core_copy(c).wait_send()
        x_copy(c).wait_send()
        for d in range(1, NZ):
            z_copy(c, d).wait_send()
            gz_copy(c, d, z).wait_send()
        return carry

    lax.fori_loop(0, chunks, finish, 0)


def fused_device(tokens, router_score, expert_ids, gate_up, down, shared_gate_up, shared_down):
    rows, width = tokens.shape
    half = rows // NX
    routed, own_shared = down.shape[1], shared_down.shape[0] // 2
    units = routed + own_shared
    steps, chunks = units // UNITS, width // WIDE
    bf16, f32 = jnp.bfloat16, jnp.float32
    any_space = pl.BlockSpec(memory_space=pl.ANY)
    vmem = pl.BlockSpec(memory_space=pltpu.VMEM)
    dma = pltpu.SemaphoreType.DMA
    out = pl.pallas_call(
        fused_kernel,
        out_shape=jax.ShapeDtypeStruct((NX, half, width), bf16),
        in_specs=[any_space, vmem, vmem] + [any_space] * 4,
        out_specs=vmem,
        scratch_shapes=[
            pltpu.VMEM((steps, width, 2 * UNITS), bf16),
            pltpu.VMEM((chunks, units, WIDE), bf16),
            pltpu.VMEM((2, 2 * rows, width), bf16),
            pltpu.VMEM((2, rows, 128), f32),
            pltpu.VMEM((steps, 2 * rows, UNITS), bf16),
            pltpu.VMEM((chunks, rows, WIDE), f32),
            pltpu.VMEM((chunks, rows, WIDE), bf16),
            pltpu.VMEM((chunks, rows, WIDE), bf16),
            pltpu.VMEM((NX, half, WIDE), f32),
            pltpu.VMEM((chunks, half, WIDE), bf16),
            pltpu.VMEM((chunks, half, WIDE), bf16),
            pltpu.VMEM((chunks, half, WIDE), f32),
            pltpu.VMEM((chunks, NZ, half, WIDE // NZ), bf16),
            pltpu.VMEM((chunks, NZ - 1, half, WIDE // NZ), bf16),
            dma((steps, 2)), dma((chunks, 2)), dma((1,)), dma((2,)), dma((2,)),
            dma((chunks,)), dma((chunks,)), dma((chunks,)), dma((chunks,)),
            dma((chunks, NZ - 1)), dma((chunks, NZ - 1)),
            dma((chunks, NZ - 1)), dma((chunks, NZ - 1)),
            dma((chunks,)), dma((chunks,)),
        ],
        compiler_params=pltpu.CompilerParams(
            collective_id=0, has_side_effects=True, vmem_limit_bytes=62 * 1024 * 1024
        ),
        name="fused_experts",
    )(
        tokens, router_score.reshape(1, rows), expert_ids, gate_up[0], down[0],
        shared_gate_up, shared_down,
    )
    return out.reshape(rows, width)


def joined_hidden(inputs, weights):
    both = jnp.dot(inputs, weights, preferred_element_type=jnp.float32)
    half_width = weights.shape[1] // 2
    return (jax.nn.silu(both[:, :half_width]) * both[:, half_width:]).astype(jnp.bfloat16)


def on_device(tokens, router_score, expert_ids, gate_up, down, shared_gate_up, shared_down):
    model_width = tokens.shape[1]
    groups_exp = lax.axis_size("expert")
    slots = groups_exp * CAP
    chosen = expert_ids[:, 0]
    member = (chosen[:, None] == jnp.arange(groups_exp, dtype=jnp.int32)[None, :]).astype(jnp.int32)
    before = jnp.cumsum(member, axis=0) - member
    target = chosen * CAP + jnp.sum(before * member, axis=1)
    placing = (jnp.arange(slots, dtype=jnp.int32)[:, None] == target[None, :]).astype(jnp.bfloat16)
    packed = jnp.dot(placing, tokens, preferred_element_type=jnp.float32).astype(jnp.bfloat16)
    packed = packed.reshape(groups_exp, CAP, model_width)
    packed_score = jnp.dot(placing, router_score[:, None], preferred_element_type=jnp.float32)
    packed_score = packed_score.astype(jnp.bfloat16).reshape(groups_exp, CAP)
    arrived, arrived_score = (
        lax.all_to_all(packed, "expert", split_axis=0, concat_axis=0, tiled=True),
        lax.all_to_all(packed_score, "expert", split_axis=0, concat_axis=0, tiled=True),
    )
    inputs = arrived.reshape(slots, model_width)
    factor = jax.nn.sigmoid(arrived_score.reshape(slots, 1).astype(jnp.float32))
    scaled = (inputs.astype(jnp.float32) * factor).astype(jnp.bfloat16)
    routed_hidden = joined_hidden(scaled, gate_up[0])
    shared_hidden = joined_hidden(inputs, shared_gate_up)
    returned = None
    result = None
    routed_part = jnp.dot(routed_hidden, down[0], preferred_element_type=jnp.float32)
    result = lax.psum(
        routed_part + jnp.dot(shared_hidden, shared_down, preferred_element_type=jnp.float32),
        "tensor",
    ).astype(jnp.bfloat16)
    returned = lax.all_to_all(
        result.reshape(groups_exp, CAP, model_width),
        "expert",
        split_axis=0,
        concat_axis=0,
        tiled=True,
    )
    mixed = jnp.dot(
        placing.T, returned.reshape(slots, model_width), preferred_element_type=jnp.float32
    )
    return mixed.astype(jnp.bfloat16)


def fits_kernel(mesh):
    return dict(mesh.shape) == {"groups": 2, "expert": 2, "tensor": NZ * NX}


def solution(mesh):
    placed = (
        P(("groups", "expert"), None),
        P(("groups", "expert")),
        P(("groups", "expert"), None),
        P("expert", None, "tensor"),
        P("expert", "tensor", None),
        P(None, "tensor"),
        P("tensor", None),
    )
    return jax.shard_map(
        fused_device if fits_kernel(mesh) else on_device,
        mesh=mesh,
        in_specs=placed,
        out_specs=P(("groups", "expert"), None),
        check_vma=False,
    )
```

```python
import jax
import jax.numpy as jnp
from jax import lax
from jax.experimental import pallas as pl
from jax.experimental.pallas import tpu as pltpu
from jax.sharding import PartitionSpec as P

CAP = 64
MESH = pl.DeviceIdType.MESH
UNITS = 256
WIDE = 512
NZ, NX = 4, 2


def fused_kernel(
    tok_ref, score_ref, ids_ref, gu_ref, down_ref, sgu_ref, sdown_ref, out_ref,
    w1, w2, lhs, aux, hidden, part, core_out, core_in, xsum, x_out, x_in, zsum, z_out, z_in,
    w1_sem, w2_sem, tok_sem, tok_send, tok_recv,
    core_send, core_recv, x_send, x_recv, z_send, z_recv, m_send, m_recv, g_send, g_recv, gx_send, gx_recv,
):
    rows, width = tok_ref.shape
    half = rows // NX
    routed = gu_ref.shape[1] // 2
    shared = sgu_ref.shape[1] // 2
    own_shared = shared // 2
    first_steps = w1.shape[0]
    chunks = w2.shape[0]
    me = lax.axis_index("expert")
    tensor = lax.axis_index("tensor")
    z, x = tensor // NX, lax.rem(tensor, NX)
    core = {"expert": 1 - me}
    xpeer = {"tensor": z * NX + 1 - x}
    inner = jnp.logical_or(z == 1, z == 2)
    zpeer = {"tensor": (z + 1 - 2 * lax.rem(z, 2)) * NX + x}
    mpeer = {"tensor": (NZ - 1 - z) * NX + x}

    def w1_copies(j):
        if j == 0:
            at = pl.multiple_of(me * own_shared, own_shared)
            pair = (sgu_ref.at[:, pl.ds(at, UNITS)], sgu_ref.at[:, pl.ds(shared + at, UNITS)])
        else:
            at = (j - 1) * UNITS
            pair = (gu_ref.at[:, pl.ds(at, UNITS)], gu_ref.at[:, pl.ds(routed + at, UNITS)])
        return [
            pltpu.make_async_copy(src, w1.at[j, :, pl.ds(i * UNITS, UNITS)], w1_sem.at[j, i])
            for i, src in enumerate(pair)
        ]

    def w2_copies(c):
        cols = pl.ds(c * WIDE, WIDE)
        at = pl.multiple_of(me * own_shared, own_shared)
        return [
            pltpu.make_async_copy(down_ref.at[:, cols], w2.at[c, pl.ds(0, routed)], w2_sem.at[c, 0]),
            pltpu.make_async_copy(
                sdown_ref.at[pl.ds(at, own_shared), cols],
                w2.at[c, pl.ds(routed, own_shared)],
                w2_sem.at[c, 1],
            ),
        ]

    own_tok = pltpu.make_async_copy(tok_ref, lhs.at[0, pl.ds(0, rows)], tok_sem.at[0])
    own_tok.start()
    for j in range(first_steps):
        for copy in w1_copies(j):
            copy.start()

    score = score_ref[...].astype(jnp.float32)
    diagonal = lax.broadcasted_iota(jnp.int32, (rows, rows), 0) == lax.broadcasted_iota(
        jnp.int32, (rows, rows), 1
    )
    score = jnp.sum(jnp.where(diagonal, score, 0.0), axis=1, keepdims=True)
    ids = jnp.where(diagonal, ids_ref[...].astype(jnp.float32), 0.0)
    ids = jnp.sum(ids, axis=1, keepdims=True)
    factor = 1.0 / (1.0 + jnp.exp(-score))
    lane = lax.broadcasted_iota(jnp.int32, (rows, 128), 1)
    aux[0] = jnp.where(lane == 0, factor, ids)

    barrier = pltpu.get_barrier_semaphore()
    for peer in (core, xpeer, zpeer, mpeer):
        pl.semaphore_signal(barrier, inc=1, device_id=peer, device_id_type=MESH)
    pl.semaphore_wait(barrier, 4)

    def remote(src, dst, send, recv, peer):
        return pltpu.make_async_remote_copy(
            src_ref=src, dst_ref=dst, send_sem=send, recv_sem=recv, device_id=peer,
            device_id_type=MESH,
        )

    tok_copy = remote(tok_ref, lhs.at[0, pl.ds(rows, rows)], tok_send.at[0], tok_recv.at[0], core)
    aux_copy = remote(aux.at[0], aux.at[1], tok_send.at[1], tok_recv.at[1], core)
    aux_copy.start()
    tok_copy.start()

    def scale(which):
        col = aux[which, :, 0:1]

        def body(i, carry):
            cols = pl.ds(pl.multiple_of(i * 512, 512), 512)
            at = pl.ds(which * rows, rows)
            lhs[1, at, cols] = (lhs[0, at, cols].astype(jnp.float32) * col).astype(jnp.bfloat16)
            return carry

        lax.fori_loop(0, width // 512, body, 0)

    own_tok.wait()
    scale(0)
    for c in range(chunks):
        for copy in w2_copies(c):
            copy.start()
    aux_copy.wait()
    tok_copy.wait()
    scale(1)

    mine = jnp.concatenate([aux[0, :, 1:2], aux[1, :, 1:2]], axis=0) == me.astype(jnp.float32)

    def first(j, carry):
        for i in range(2):
            block = w1.at[j, :, pl.ds(i * UNITS, UNITS)]
            pltpu.make_async_copy(block, block, w1_sem.at[j, i]).wait()
        both = jnp.dot(lhs[jnp.minimum(j, 1)], w1[j], preferred_element_type=jnp.float32)
        gate, up = both[:, :UNITS], both[:, UNITS:]
        unit = gate / (1.0 + jnp.exp(-gate)) * up
        unit = jnp.where(jnp.logical_or(mine, j == 0), unit, 0.0)
        hidden[j] = unit.astype(jnp.bfloat16)
        return carry

    lax.fori_loop(0, first_steps, first, 0)

    def core_copy(c):
        return remote(core_out.at[c], core_in.at[c], core_send.at[c], core_recv.at[c], core)

    def x_copy(c):
        return remote(x_out.at[c], x_in.at[c], x_send.at[c], x_recv.at[c], xpeer)

    def z_copy(c):
        return remote(z_out.at[c], z_in.at[0, c], z_send.at[c], z_recv.at[c], zpeer)

    def m_copy(c):
        return remote(z_out.at[c], z_in.at[1, c], m_send.at[c], m_recv.at[c], mpeer)

    def columns(c):
        return pl.ds(pl.multiple_of(c * WIDE, WIDE), WIDE)

    def g_copy(c):
        block = out_ref.at[x, :, columns(c)]
        return remote(block, block, g_send.at[c], g_recv.at[c], zpeer)

    def gx_copy(c, side):
        block = out_ref.at[side, :, columns(c)]
        return remote(block, block, gx_send.at[c], gx_recv.at[c], xpeer)

    def second(c):
        for i, (at, size) in enumerate(((0, routed), (routed, own_shared))):
            block = w2.at[c, pl.ds(at, size)]
            pltpu.make_async_copy(block, block, w2_sem.at[c, i]).wait()
        for n in range(WIDE // 512):
            cols = pl.ds(n * 512, 512)
            total = None
            for j in range(first_steps):
                at = routed if j == 0 else (j - 1) * UNITS
                term = jnp.dot(
                    hidden[j], w2[c, pl.ds(at, UNITS), cols], preferred_element_type=jnp.float32
                )
                total = term if total is None else total + term
            part[c, :, cols] = total[:rows]
            core_out[c, :, cols] = total[rows:].astype(jnp.bfloat16)
        core_copy(c).start()

    def join_cores(c):
        core_copy(c).wait_recv()
        total = part[c] + core_in[c].astype(jnp.float32)
        xsum[0] = total[:half]
        xsum[1] = total[half:]
        zsum[c] = xsum[x]
        x_out[c] = xsum[1 - x].astype(jnp.bfloat16)
        x_copy(c).start()

    def join_x(c):
        x_copy(c).wait_recv()
        total = zsum[c] + x_in[c].astype(jnp.float32)

        @pl.when(inner)
        def _():
            zsum[c] = total

        @pl.when(jnp.logical_not(inner))
        def _():
            z_out[c] = total.astype(jnp.bfloat16)
            z_copy(c).start()

    def join_z(c):
        @pl.when(inner)
        def _():
            z_copy(c).wait_recv()
            z_out[c] = (zsum[c] + z_in[0, c].astype(jnp.float32)).astype(jnp.bfloat16)
            m_copy(c).start()

    def join_middle(c):
        @pl.when(inner)
        def _():
            m_copy(c).wait_recv()
            total = z_out[c].astype(jnp.float32) + z_in[1, c].astype(jnp.float32)
            out_ref[x, :, columns(c)] = total.astype(jnp.bfloat16)
            g_copy(c).start()
            gx_copy(c, x).start()

    def pass_x(c):
        @pl.when(jnp.logical_not(inner))
        def _():
            g_copy(c).wait_recv()
            gx_copy(c, x).start()

    stages = ((0, second), (2, join_cores), (5, join_x), (8, join_z), (11, join_middle), (14, pass_x))

    def step(s, carry):
        for lag, stage in stages:
            c = s - lag

            @pl.when(jnp.logical_and(c >= 0, c < chunks))
            def _(stage=stage, c=c):
                stage(c)

        return carry

    lax.fori_loop(0, chunks + stages[-1][0], step, 0)

    def finish(c, carry):
        gx_copy(c, 1 - x).wait_recv()
        gx_copy(c, x).wait_send()
        core_copy(c).wait_send()
        x_copy(c).wait_send()

        @pl.when(inner)
        def _():
            m_copy(c).wait_send()
            g_copy(c).wait_send()

        @pl.when(jnp.logical_not(inner))
        def _():
            z_copy(c).wait_send()

        return carry

    lax.fori_loop(0, chunks, finish, 0)


def fused_device(tokens, router_score, expert_ids, gate_up, down, shared_gate_up, shared_down):
    rows, width = tokens.shape
    half = rows // NX
    routed, own_shared = down.shape[1], shared_down.shape[0] // 2
    units = routed + own_shared
    steps, chunks = units // UNITS, width // WIDE
    bf16, f32 = jnp.bfloat16, jnp.float32
    any_space = pl.BlockSpec(memory_space=pl.ANY)
    vmem = pl.BlockSpec(memory_space=pltpu.VMEM)
    dma = pltpu.SemaphoreType.DMA
    out = pl.pallas_call(
        fused_kernel,
        out_shape=jax.ShapeDtypeStruct((NX, half, width), bf16),
        in_specs=[any_space, vmem, vmem] + [any_space] * 4,
        out_specs=vmem,
        scratch_shapes=[
            pltpu.VMEM((steps, width, 2 * UNITS), bf16),
            pltpu.VMEM((chunks, units, WIDE), bf16),
            pltpu.VMEM((2, 2 * rows, width), bf16),
            pltpu.VMEM((2, rows, 128), f32),
            pltpu.VMEM((steps, 2 * rows, UNITS), bf16),
            pltpu.VMEM((chunks, rows, WIDE), f32),
            pltpu.VMEM((chunks, rows, WIDE), bf16),
            pltpu.VMEM((chunks, rows, WIDE), bf16),
            pltpu.VMEM((NX, half, WIDE), f32),
            pltpu.VMEM((chunks, half, WIDE), bf16),
            pltpu.VMEM((chunks, half, WIDE), bf16),
            pltpu.VMEM((chunks, half, WIDE), f32),
            pltpu.VMEM((chunks, half, WIDE), bf16),
            pltpu.VMEM((2, chunks, half, WIDE), bf16),
            dma((steps, 2)), dma((chunks, 2)), dma((1,)), dma((2,)), dma((2,)),
            dma((chunks,)), dma((chunks,)), dma((chunks,)), dma((chunks,)),
            dma((chunks,)), dma((chunks,)), dma((chunks,)), dma((chunks,)),
            dma((chunks,)), dma((chunks,)), dma((chunks,)), dma((chunks,)),
        ],
        compiler_params=pltpu.CompilerParams(
            collective_id=0, has_side_effects=True, vmem_limit_bytes=62 * 1024 * 1024
        ),
        name="fused_experts",
    )(
        tokens, router_score.reshape(1, rows), expert_ids.reshape(1, rows), gate_up[0], down[0],
        shared_gate_up, shared_down,
    )
    return out.reshape(rows, width)


def joined_hidden(inputs, weights):
    both = jnp.dot(inputs, weights, preferred_element_type=jnp.float32)
    half_width = weights.shape[1] // 2
    return (jax.nn.silu(both[:, :half_width]) * both[:, half_width:]).astype(jnp.bfloat16)


def on_device(tokens, router_score, expert_ids, gate_up, down, shared_gate_up, shared_down):
    model_width = tokens.shape[1]
    groups_exp = lax.axis_size("expert")
    slots = groups_exp * CAP
    chosen = expert_ids[:, 0]
    member = (chosen[:, None] == jnp.arange(groups_exp, dtype=jnp.int32)[None, :]).astype(jnp.int32)
    before = jnp.cumsum(member, axis=0) - member
    target = chosen * CAP + jnp.sum(before * member, axis=1)
    placing = (jnp.arange(slots, dtype=jnp.int32)[:, None] == target[None, :]).astype(jnp.bfloat16)
    packed = jnp.dot(placing, tokens, preferred_element_type=jnp.float32).astype(jnp.bfloat16)
    packed = packed.reshape(groups_exp, CAP, model_width)
    packed_score = jnp.dot(placing, router_score[:, None], preferred_element_type=jnp.float32)
    packed_score = packed_score.astype(jnp.bfloat16).reshape(groups_exp, CAP)
    arrived, arrived_score = (
        lax.all_to_all(packed, "expert", split_axis=0, concat_axis=0, tiled=True),
        lax.all_to_all(packed_score, "expert", split_axis=0, concat_axis=0, tiled=True),
    )
    inputs = arrived.reshape(slots, model_width)
    factor = jax.nn.sigmoid(arrived_score.reshape(slots, 1).astype(jnp.float32))
    scaled = (inputs.astype(jnp.float32) * factor).astype(jnp.bfloat16)
    routed_hidden = joined_hidden(scaled, gate_up[0])
    shared_hidden = joined_hidden(inputs, shared_gate_up)
    returned = None
    result = None
    routed_part = jnp.dot(routed_hidden, down[0], preferred_element_type=jnp.float32)
    result = lax.psum(
        routed_part + jnp.dot(shared_hidden, shared_down, preferred_element_type=jnp.float32),
        "tensor",
    ).astype(jnp.bfloat16)
    returned = lax.all_to_all(
        result.reshape(groups_exp, CAP, model_width),
        "expert",
        split_axis=0,
        concat_axis=0,
        tiled=True,
    )
    mixed = jnp.dot(
        placing.T, returned.reshape(slots, model_width), preferred_element_type=jnp.float32
    )
    return mixed.astype(jnp.bfloat16)


def fits_kernel(mesh):
    return dict(mesh.shape) == {"groups": 2, "expert": 2, "tensor": NZ * NX}


def solution(mesh):
    placed = (
        P(("groups", "expert"), None),
        P(("groups", "expert")),
        P(("groups", "expert"), None),
        P("expert", None, "tensor"),
        P("expert", "tensor", None),
        P(None, "tensor"),
        P("tensor", None),
    )
    return jax.shard_map(
        fused_device if fits_kernel(mesh) else on_device,
        mesh=mesh,
        in_specs=placed,
        out_specs=P(("groups", "expert"), None),
        check_vma=False,
    )
```

```python
import jax
import jax.numpy as jnp
from jax import lax
from jax.experimental import pallas as pl
from jax.experimental.pallas import tpu as pltpu
from jax.sharding import PartitionSpec as P

CAP = 64
MESH = pl.DeviceIdType.MESH
UNITS = 256
WIDE = 512
NZ, NX = 4, 2


def fused_kernel(
    tok_ref, score_ref, ids_ref, gu_ref, down_ref, sgu_ref, sdown_ref, out_ref,
    w1, w2, lhs, aux, hidden, part, core_out, core_in, xsum, x_out, x_in, zsum, z_out, z_in,
    w1_sem, w2_sem, tok_sem, tok_send, tok_recv,
    core_send, core_recv, x_send, x_recv, z_send, z_recv, m_send, m_recv, g_send, g_recv, gx_send, gx_recv,
):
    rows, width = tok_ref.shape
    half = rows // NX
    routed = gu_ref.shape[1] // 2
    shared = sgu_ref.shape[1] // 2
    own_shared = shared // 2
    first_steps = w1.shape[0]
    chunks = w2.shape[0]
    me = lax.axis_index("expert")
    tensor = lax.axis_index("tensor")
    z, x = tensor // NX, lax.rem(tensor, NX)
    core = {"expert": 1 - me}
    xpeer = {"tensor": z * NX + 1 - x}
    inner = jnp.logical_or(z == 1, z == 2)
    zpeer = {"tensor": (z + 1 - 2 * lax.rem(z, 2)) * NX + x}
    mpeer = {"tensor": (NZ - 1 - z) * NX + x}

    def w1_copies(j):
        if j == 0:
            at = pl.multiple_of(me * own_shared, own_shared)
            pair = (sgu_ref.at[:, pl.ds(at, UNITS)], sgu_ref.at[:, pl.ds(shared + at, UNITS)])
        else:
            at = (j - 1) * UNITS
            pair = (gu_ref.at[:, pl.ds(at, UNITS)], gu_ref.at[:, pl.ds(routed + at, UNITS)])
        return [
            pltpu.make_async_copy(src, w1.at[j, :, pl.ds(i * UNITS, UNITS)], w1_sem.at[j, i])
            for i, src in enumerate(pair)
        ]

    def w2_copies(c):
        cols = pl.ds(c * WIDE, WIDE)
        at = pl.multiple_of(me * own_shared, own_shared)
        return [
            pltpu.make_async_copy(down_ref.at[:, cols], w2.at[c, pl.ds(0, routed)], w2_sem.at[c, 0]),
            pltpu.make_async_copy(
                sdown_ref.at[pl.ds(at, own_shared), cols],
                w2.at[c, pl.ds(routed, own_shared)],
                w2_sem.at[c, 1],
            ),
        ]

    own_tok = pltpu.make_async_copy(tok_ref, lhs.at[0, pl.ds(0, rows)], tok_sem.at[0])
    own_tok.start()
    for j in range(first_steps):
        for copy in w1_copies(j):
            copy.start()

    score = score_ref[...].astype(jnp.float32)
    diagonal = lax.broadcasted_iota(jnp.int32, (rows, rows), 0) == lax.broadcasted_iota(
        jnp.int32, (rows, rows), 1
    )
    score = jnp.sum(jnp.where(diagonal, score, 0.0), axis=1, keepdims=True)
    ids = jnp.where(diagonal, ids_ref[...].astype(jnp.float32), 0.0)
    ids = jnp.sum(ids, axis=1, keepdims=True)
    factor = 1.0 / (1.0 + jnp.exp(-score))
    lane = lax.broadcasted_iota(jnp.int32, (rows, 128), 1)
    aux[0] = jnp.where(lane == 0, factor, ids)

    barrier = pltpu.get_barrier_semaphore()
    for peer in (core, xpeer, zpeer, mpeer):
        pl.semaphore_signal(barrier, inc=1, device_id=peer, device_id_type=MESH)
    pl.semaphore_wait(barrier, 4)

    def remote(src, dst, send, recv, peer):
        return pltpu.make_async_remote_copy(
            src_ref=src, dst_ref=dst, send_sem=send, recv_sem=recv, device_id=peer,
            device_id_type=MESH,
        )

    tok_copy = remote(tok_ref, lhs.at[0, pl.ds(rows, rows)], tok_send.at[0], tok_recv.at[0], core)
    aux_copy = remote(aux.at[0], aux.at[1], tok_send.at[1], tok_recv.at[1], core)
    aux_copy.start()
    tok_copy.start()

    def scale(which):
        col = aux[which, :, 0:1]

        def body(i, carry):
            cols = pl.ds(pl.multiple_of(i * 512, 512), 512)
            at = pl.ds(which * rows, rows)
            lhs[1, at, cols] = (lhs[0, at, cols].astype(jnp.float32) * col).astype(jnp.bfloat16)
            return carry

        lax.fori_loop(0, width // 512, body, 0)

    own_tok.wait()
    scale(0)
    for c in range(chunks):
        for copy in w2_copies(c):
            copy.start()
    aux_copy.wait()
    tok_copy.wait()
    scale(1)

    mine = jnp.concatenate([aux[0, :, 1:2], aux[1, :, 1:2]], axis=0) == me.astype(jnp.float32)

    def first(j, carry):
        for i in range(2):
            block = w1.at[j, :, pl.ds(i * UNITS, UNITS)]
            pltpu.make_async_copy(block, block, w1_sem.at[j, i]).wait()
        both = jnp.dot(lhs[jnp.minimum(j, 1)], w1[j], preferred_element_type=jnp.float32)
        gate, up = both[:, :UNITS], both[:, UNITS:]
        unit = gate / (1.0 + jnp.exp(-gate)) * up
        unit = jnp.where(jnp.logical_or(mine, j == 0), unit, 0.0)
        hidden[j] = unit.astype(jnp.bfloat16)
        return carry

    lax.fori_loop(0, first_steps, first, 0)

    def core_copy(c):
        return remote(core_out.at[c], core_in.at[c], core_send.at[c], core_recv.at[c], core)

    def x_copy(c):
        return remote(x_out.at[c], x_in.at[c], x_send.at[c], x_recv.at[c], xpeer)

    def z_copy(c):
        return remote(z_out.at[c], z_in.at[0, c], z_send.at[c], z_recv.at[c], zpeer)

    def m_copy(c):
        return remote(z_out.at[c], z_in.at[1, c], m_send.at[c], m_recv.at[c], mpeer)

    def columns(c):
        return pl.ds(pl.multiple_of(c * WIDE, WIDE), WIDE)

    def g_copy(c):
        block = out_ref.at[x, :, columns(c)]
        return remote(block, block, g_send.at[c], g_recv.at[c], zpeer)

    def gx_copy(c, side):
        block = out_ref.at[side, :, columns(c)]
        return remote(block, block, gx_send.at[c], gx_recv.at[c], xpeer)

    def second(c):
        for i, (at, size) in enumerate(((0, routed), (routed, own_shared))):
            block = w2.at[c, pl.ds(at, size)]
            pltpu.make_async_copy(block, block, w2_sem.at[c, i]).wait()
        for n in range(WIDE // 512):
            cols = pl.ds(n * 512, 512)
            total = None
            for j in range(first_steps):
                at = routed if j == 0 else (j - 1) * UNITS
                term = jnp.dot(
                    hidden[j], w2[c, pl.ds(at, UNITS), cols], preferred_element_type=jnp.float32
                )
                total = term if total is None else total + term
            part[c, :, cols] = total[:rows]
            core_out[c, :, cols] = total[rows:].astype(jnp.bfloat16)
        core_copy(c).start()

    def join_cores(c):
        core_copy(c).wait_recv()
        total = part[c] + core_in[c].astype(jnp.float32)
        xsum[0] = total[:half]
        xsum[1] = total[half:]
        zsum[c] = xsum[x]
        x_out[c] = xsum[1 - x].astype(jnp.bfloat16)
        x_copy(c).start()

    def join_x(c):
        x_copy(c).wait_recv()
        total = zsum[c] + x_in[c].astype(jnp.float32)

        @pl.when(inner)
        def _():
            zsum[c] = total

        @pl.when(jnp.logical_not(inner))
        def _():
            z_out[c] = total.astype(jnp.bfloat16)
            z_copy(c).start()

    def join_z(c):
        @pl.when(inner)
        def _():
            z_copy(c).wait_recv()
            z_out[c] = (zsum[c] + z_in[0, c].astype(jnp.float32)).astype(jnp.bfloat16)
            m_copy(c).start()

    def join_middle(c):
        @pl.when(inner)
        def _():
            m_copy(c).wait_recv()
            total = z_out[c].astype(jnp.float32) + z_in[1, c].astype(jnp.float32)
            out_ref[x, :, columns(c)] = total.astype(jnp.bfloat16)
            g_copy(c).start()
            gx_copy(c, x).start()

    def pass_x(c):
        @pl.when(jnp.logical_not(inner))
        def _():
            g_copy(c).wait_recv()
            gx_copy(c, x).start()

    stages = ((0, second), (2, join_cores), (5, join_x), (8, join_z), (11, join_middle), (14, pass_x))

    def step(s, carry):
        for lag, stage in stages:
            c = s - lag

            @pl.when(jnp.logical_and(c >= 0, c < chunks))
            def _(stage=stage, c=c):
                stage(c)

        return carry

    lax.fori_loop(0, chunks + stages[-1][0], step, 0)

    def finish(c, carry):
        gx_copy(c, 1 - x).wait_recv()
        gx_copy(c, x).wait_send()
        core_copy(c).wait_send()
        x_copy(c).wait_send()

        @pl.when(inner)
        def _():
            m_copy(c).wait_send()
            g_copy(c).wait_send()

        @pl.when(jnp.logical_not(inner))
        def _():
            z_copy(c).wait_send()

        return carry

    lax.fori_loop(0, chunks, finish, 0)


def fused_device(tokens, router_score, expert_ids, gate_up, down, shared_gate_up, shared_down):
    rows, width = tokens.shape
    half = rows // NX
    routed, own_shared = down.shape[1], shared_down.shape[0] // 2
    units = routed + own_shared
    steps, chunks = units // UNITS, width // WIDE
    bf16, f32 = jnp.bfloat16, jnp.float32
    any_space = pl.BlockSpec(memory_space=pl.ANY)
    vmem = pl.BlockSpec(memory_space=pltpu.VMEM)
    dma = pltpu.SemaphoreType.DMA
    out = pl.pallas_call(
        fused_kernel,
        out_shape=jax.ShapeDtypeStruct((NX, half, width), bf16),
        in_specs=[any_space, vmem, vmem] + [any_space] * 4,
        out_specs=vmem,
        scratch_shapes=[
            pltpu.VMEM((steps, width, 2 * UNITS), bf16),
            pltpu.VMEM((chunks, units, WIDE), bf16),
            pltpu.VMEM((2, 2 * rows, width), bf16),
            pltpu.VMEM((2, rows, 128), f32),
            pltpu.VMEM((steps, 2 * rows, UNITS), bf16),
            pltpu.VMEM((chunks, rows, WIDE), f32),
            pltpu.VMEM((chunks, rows, WIDE), bf16),
            pltpu.VMEM((chunks, rows, WIDE), bf16),
            pltpu.VMEM((NX, half, WIDE), f32),
            pltpu.VMEM((chunks, half, WIDE), bf16),
            pltpu.VMEM((chunks, half, WIDE), bf16),
            pltpu.VMEM((chunks, half, WIDE), f32),
            pltpu.VMEM((chunks, half, WIDE), bf16),
            pltpu.VMEM((2, chunks, half, WIDE), bf16),
            dma((steps, 2)), dma((chunks, 2)), dma((1,)), dma((2,)), dma((2,)),
            dma((chunks,)), dma((chunks,)), dma((chunks,)), dma((chunks,)),
            dma((chunks,)), dma((chunks,)), dma((chunks,)), dma((chunks,)),
            dma((chunks,)), dma((chunks,)), dma((chunks,)), dma((chunks,)),
        ],
        compiler_params=pltpu.CompilerParams(
            collective_id=0, has_side_effects=True, vmem_limit_bytes=52 * 1024 * 1024
        ),
        name="fused_experts",
    )(
        tokens, router_score.reshape(1, rows), expert_ids.reshape(1, rows), gate_up[0], down[0],
        shared_gate_up, shared_down,
    )
    return out.reshape(rows, width)


def joined_hidden(inputs, weights):
    both = jnp.dot(inputs, weights, preferred_element_type=jnp.float32)
    half_width = weights.shape[1] // 2
    return (jax.nn.silu(both[:, :half_width]) * both[:, half_width:]).astype(jnp.bfloat16)


def on_device(tokens, router_score, expert_ids, gate_up, down, shared_gate_up, shared_down):
    model_width = tokens.shape[1]
    groups_exp = lax.axis_size("expert")
    slots = groups_exp * CAP
    chosen = expert_ids[:, 0]
    member = (chosen[:, None] == jnp.arange(groups_exp, dtype=jnp.int32)[None, :]).astype(jnp.int32)
    before = jnp.cumsum(member, axis=0) - member
    target = chosen * CAP + jnp.sum(before * member, axis=1)
    placing = (jnp.arange(slots, dtype=jnp.int32)[:, None] == target[None, :]).astype(jnp.bfloat16)
    packed = jnp.dot(placing, tokens, preferred_element_type=jnp.float32).astype(jnp.bfloat16)
    packed = packed.reshape(groups_exp, CAP, model_width)
    packed_score = jnp.dot(placing, router_score[:, None], preferred_element_type=jnp.float32)
    packed_score = packed_score.astype(jnp.bfloat16).reshape(groups_exp, CAP)
    arrived, arrived_score = (
        lax.all_to_all(packed, "expert", split_axis=0, concat_axis=0, tiled=True),
        lax.all_to_all(packed_score, "expert", split_axis=0, concat_axis=0, tiled=True),
    )
    inputs = arrived.reshape(slots, model_width)
    factor = jax.nn.sigmoid(arrived_score.reshape(slots, 1).astype(jnp.float32))
    scaled = (inputs.astype(jnp.float32) * factor).astype(jnp.bfloat16)
    routed_hidden = joined_hidden(scaled, gate_up[0])
    shared_hidden = joined_hidden(inputs, shared_gate_up)
    returned = None
    result = None
    routed_part = jnp.dot(routed_hidden, down[0], preferred_element_type=jnp.float32)
    result = lax.psum(
        routed_part + jnp.dot(shared_hidden, shared_down, preferred_element_type=jnp.float32),
        "tensor",
    ).astype(jnp.bfloat16)
    returned = lax.all_to_all(
        result.reshape(groups_exp, CAP, model_width),
        "expert",
        split_axis=0,
        concat_axis=0,
        tiled=True,
    )
    mixed = jnp.dot(
        placing.T, returned.reshape(slots, model_width), preferred_element_type=jnp.float32
    )
    return mixed.astype(jnp.bfloat16)


def fits_kernel(mesh):
    return dict(mesh.shape) == {"groups": 2, "expert": 2, "tensor": NZ * NX}


def solution(mesh):
    placed = (
        P(("groups", "expert"), None),
        P(("groups", "expert")),
        P(("groups", "expert"), None),
        P("expert", None, "tensor"),
        P("expert", "tensor", None),
        P(None, "tensor"),
        P("tensor", None),
    )
    return jax.shard_map(
        fused_device if fits_kernel(mesh) else on_device,
        mesh=mesh,
        in_specs=placed,
        out_specs=P(("groups", "expert"), None),
        check_vma=False,
    )
```
